32 devices in a mesh: feat: 2 (over x), rows: 16 (over z, y, core).
Axes of the slice: x: 2, y: 2, z: 4, core: 2. Of those that a mesh axis runs over, the one named last changes fastest.
Arguments:
- features: bfloat16 [16384, 4096], P('rows', 'feat'), may hold values from -6 to 6
- coeffs: float32 [4096, 96], P(('feat', 'rows')), may hold values from -0.09375 to 0.09375
- inverse: float32 [4096, 2048], P(('feat', 'rows')), as said below
- labels: int32 [16384], P('rows'), may hold values from 0 to 95
Outputs:
- new_coeffs: float32 [4096, 96], P(('feat', 'rows'))
- block_residuals: float32 [2, 16384, 96], P('feat', 'rows')
- residual_norms: float32 [2, 96], P('feat')
The draws below stay inside these ranges and needn't reach their ends.
Inputs may be any that keep to these rules, and one draw needn't show every extreme that they name: Each block of 2048 rows of inverse is a symmetric matrix.
All inputs are finite; a program needn't handle non-finite values.
Results may differ from the reference program's by a relative error of at most 0.0036.
Values may be sent and summed in bfloat16 or wider, within the bound.
No kernel may reach another device: no remote copies, remote signals or barrier semaphores. Data moves between devices by JAX's collectives and lax.ppermute only.
A program may use at most 64 MiB of HBM per device.

```python
import jax
import jax.numpy as jnp
from jax import lax

BW = 2048
CLASSES = 96
ROWS = 16384
FEATS = 4096
N_FEAT = 2


def draw_inverse(key, part):
    key = jax.random.fold_in(key, 7)
    key_diag, key_noise = jax.random.split(key)
    noise = jax.random.normal(key_noise, (N_FEAT, BW, BW), jnp.float32)
    sym = (noise + jnp.swapaxes(noise, 1, 2)) * (0.15 / (2.0 * BW) ** 0.5)
    diag = jax.random.uniform(key_diag, (N_FEAT, BW, 1), jnp.float32, 0.6, 1.0)
    eye = jnp.eye(BW, dtype=jnp.float32)[None, :, :]
    whole = (diag * eye + sym) * (0.5 / ROWS)
    return whole.reshape(N_FEAT * BW, BW)


def set_ends(entries, stream_key, least, largest):
    dims = entries.shape
    place = [jax.random.randint(jax.random.fold_in(stream_key, axis), (), 0, dims[axis]) for axis in range(len(dims))]
    entries = entries.at[tuple(place)].set(least)
    longest = dims.index(max(dims))
    place[longest] = (place[longest] + 1) % dims[longest]
    return entries.at[tuple(place)].set(largest)


def steps_of(stream_key, shape, cuts, smallest, high):
    factor_of, own = 1.0, jax.random.fold_in(stream_key, 6)
    for dim, parts in cuts:
        draws = jnp.exp(jax.random.uniform(jax.random.fold_in(own, dim), (parts,), jnp.float32, smallest / len(cuts), high / len(cuts)))
        factor_of = factor_of * jnp.repeat(draws, shape[dim] // parts).reshape([-1 if axis == dim else 1 for axis in range(len(shape))])
    return factor_of


def bell_draw(own_key, dims, scale, reach, cuts=(), held_as=jnp.bfloat16):
    drawn = jax.random.normal(own_key, dims, jnp.float32) * scale
    if len(cuts) > 0:
        drawn = steps_of(own_key, dims, cuts, -0.22, 0.18) * drawn
    return jnp.clip(drawn, min=-reach, max=reach).astype(held_as)


def setup_inputs(seed: int = 0) -> dict:
    streams_of = jax.random.split(jax.random.key(seed), 5)
    features = bell_draw(streams_of[0], (ROWS, FEATS), 1.0, 6.0, ((0, 16), (1, 2)))
    coeffs = bell_draw(streams_of[1], (FEATS, CLASSES), FEATS ** -0.5, 0.09375, ((0, 32),), jnp.float32)
    inverse = draw_inverse(jax.random.fold_in(streams_of[4], 71), 0)
    labels = set_ends(jax.random.randint(streams_of[3], (ROWS,), 0, CLASSES), jax.random.fold_in(streams_of[3], 1), 0, CLASSES - 1).astype(jnp.int32)
    return {"features": features, "coeffs": coeffs, "inverse": inverse, "labels": labels}


def reference(features, coeffs, inverse, labels):
    high = lax.Precision.HIGHEST
    targets = (labels[:, None] == jnp.arange(CLASSES, dtype=jnp.int32)[None, :]).astype(jnp.float32)
    fitted = jnp.zeros((ROWS, CLASSES), jnp.float32)
    for block in range(N_FEAT):
        zfull = features[:, block * BW:(block + 1) * BW].astype(jnp.float32)
        wlow = lax.optimization_barrier(coeffs[block * BW:(block + 1) * BW].astype(jnp.bfloat16)).astype(jnp.float32)
        fitted = fitted + jnp.dot(zfull, wlow, precision=high)
    residual = targets - fitted
    new_rows = []
    kept = []
    norms = []
    for block in range(N_FEAT):
        zfull = features[:, block * BW:(block + 1) * BW].astype(jnp.float32)
        rlow = lax.optimization_barrier(residual.astype(jnp.bfloat16)).astype(jnp.float32)
        grad = jnp.dot(zfull.T, rlow, precision=high)
        delta = jnp.dot(inverse[block * BW:(block + 1) * BW], grad, precision=high)
        new_rows.append(coeffs[block * BW:(block + 1) * BW] + delta)
        dlow = lax.optimization_barrier(delta.astype(jnp.bfloat16)).astype(jnp.float32)
        residual = residual - jnp.dot(zfull, dlow, precision=high)
        kept.append(residual)
        norms.append(jnp.sum(residual * residual, axis=0))
    return jnp.concatenate(new_rows, axis=0), jnp.stack(kept), jnp.stack(norms)
```

```python
import jax
import jax.numpy as jnp
from jax import lax
from jax.sharding import PartitionSpec as P

LOW = jnp.bfloat16
WIDE = jnp.float32


def swapped(shard, axis, bit):
    peers = lax.axis_size(axis)
    return lax.ppermute(shard, axis, [(i, i ^ bit) for i in range(peers)])


def split(wide):
    high = lax.reduce_precision(wide, 8, 7)
    return high.astype(LOW), (wide - high).astype(LOW)


def on_device(features, coeffs, inverse, labels):
    nfeat = lax.axis_size("feat")
    nrows = lax.axis_size("rows")
    block = lax.axis_index("feat")
    me = lax.axis_index("rows")
    own, classes = coeffs.shape
    width = features.shape[1]
    inner = 4
    outer = nrows // inner
    low_bit, next_bit = me % 2, (me // 2) % 2
    same_low = [[bit + 2 * k for k in range(nrows // 2)] for bit in range(2)]
    same_inner = [[k + inner * z for z in range(outer)] for k in range(inner)]

    def both(mine, axis_at):
        other = swapped(mine, "rows", 1)
        first = jnp.where(low_bit == 0, mine, other)
        second = jnp.where(low_bit == 0, other, mine)
        return jnp.stack([first, second], axis=axis_at)

    def halves(whole, bit, axis_at):
        keep = lax.dynamic_index_in_dim(whole, bit, axis_at, keepdims=False)
        send = lax.dynamic_index_in_dim(whole, 1 - bit, axis_at, keepdims=False)
        return keep, send

    inverse_low = lax.all_gather(
        inverse.astype(LOW), "rows", axis=0, axis_index_groups=same_inner, tiled=True
    )

    coeffs_low = coeffs.astype(LOW)
    from_chips = lax.all_to_all(
        jnp.broadcast_to(coeffs_low[None], (nrows // 2, own, classes)),
        "rows", 0, 0, axis_index_groups=same_low, tiled=True,
    )
    all_coeffs = both(from_chips, 1).reshape(width, classes)
    fitted = jnp.dot(features, all_coeffs, preferred_element_type=WIDE)
    bits = [1 << k for k in range((nfeat - 1).bit_length())]
    for bit in bits[:-1]:
        fitted = fitted + swapped(fitted, "feat", bit)
    fit_high, fit_rest = split(fitted)
    targets = (labels[:, None] == jnp.arange(classes, dtype=jnp.int32)[None, :]).astype(WIDE)
    near = (targets - fitted) - swapped(fit_high, "feat", bits[-1]).astype(WIDE)
    incoming_low = near.astype(LOW)
    incoming = near - swapped(fit_rest, "feat", bits[-1]).astype(WIDE)

    contract = (((0,), (0,)), ((), ()))
    kept = jnp.zeros_like(incoming)
    delta_kept = jnp.zeros_like(coeffs)
    for turn in range(nfeat):
        grad = lax.dot_general(
            features, incoming_low, contract, preferred_element_type=WIDE
        ).reshape(outer, 2, 2, own, classes)
        keep, send = halves(grad, low_bit, 2)
        grad = keep + swapped(send, "rows", 1)
        keep, send = halves(grad, next_bit, 1)
        grad = keep + swapped(send.astype(LOW), "rows", 2).astype(WIDE)
        grad_low = grad.astype(LOW)
        for z in range(1, outer):
            grad = grad + swapped(grad_low, "rows", inner * z).astype(WIDE)
        pair = jnp.concatenate(split(grad.reshape(outer * own, classes)), axis=1)
        part = lax.dot_general(inverse_low, pair, contract, preferred_element_type=WIDE)
        part = (part[:, :classes] + part[:, classes:]).reshape(outer, 2, 2, own, classes)
        keep, send = halves(part, low_bit, 2)
        part = keep + swapped(send, "rows", 1)
        delta = part + swapped(part.astype(LOW), "rows", 2).astype(WIDE)
        delta_low = both(delta.astype(LOW), 2).reshape(width, classes)
        delta_mine = lax.dynamic_index_in_dim(
            delta.reshape(nrows // 2, own, classes), me // 2, 0, keepdims=False
        )
        outgoing = incoming - jnp.dot(features, delta_low, preferred_element_type=WIDE)
        active = block == turn
        kept = jnp.where(active, outgoing, kept)
        delta_kept = jnp.where(active, delta_mine, delta_kept)
        if turn < nfeat - 1:
            along = [(i, (i + 1) % nfeat) for i in range(nfeat)]
            high, rest = split(outgoing)
            incoming_low = lax.ppermute(high, "feat", along)
            incoming = incoming_low.astype(WIDE) + lax.ppermute(rest, "feat", along).astype(WIDE)

    squares = jnp.sum(kept * kept, axis=0, keepdims=True)
    squares = lax.all_to_all(
        jnp.broadcast_to(squares[None], (nrows, 1, classes)), "rows", 0, 0, tiled=True
    )
    return (coeffs + delta_kept, kept[None], jnp.sum(squares, axis=0))


def solution(mesh):
    placed = (P("rows", "feat"), P(("feat", "rows"), None), P(("feat", "rows"), None), P("rows"))
    return jax.shard_map(
        on_device,
        mesh=mesh,
        in_specs=placed,
        out_specs=(P(("feat", "rows"), None), P("feat", "rows", None), P("feat", None)),
        check_vma=False,
    )
```

```python
import functools

import jax
import jax.numpy as jnp
from jax import lax
from jax.experimental import pallas as pl
from jax.experimental.pallas import tpu as pltpu
from jax.sharding import PartitionSpec as P

LOW = jnp.bfloat16
WIDE = jnp.float32
INNER = 4


def swapped(shard, axis, bit):
    peers = lax.axis_size(axis)
    return lax.ppermute(shard, axis, [(i, i ^ bit) for i in range(peers)])


def split(wide):
    high = lax.reduce_precision(wide, 8, 7)
    return high.astype(LOW), (wide - high).astype(LOW)


def tied(*arrays):
    return lax.optimization_barrier(arrays)


def halved(whole):
    half = whole.shape[0] // 2
    return whole[:half], whole[half:]


def reorder_kernel(order, own, me_ref, given, taken, sems):
    me = me_ref[0]
    copies = []
    for slot, code in enumerate(order):
        start = pl.multiple_of((me ^ code) * own, own)
        copies.append(
            pltpu.make_async_copy(
                given.at[:, pl.ds(start, own)], taken.at[:, pl.ds(slot * own, own)], sems.at[slot]
            )
        )
    for copy in copies:
        copy.start()
    for copy in copies:
        copy.wait()


def reordered(features, me, order, own):
    if own % 128:
        parts = [lax.dynamic_slice_in_dim(features, (me ^ code) * own, own, 1) for code in order]
        return jnp.concatenate(parts, axis=1)
    return pl.pallas_call(
        functools.partial(reorder_kernel, order, own),
        out_shape=jax.ShapeDtypeStruct(features.shape, features.dtype),
        in_specs=[pl.BlockSpec(memory_space=pltpu.SMEM), pl.BlockSpec(memory_space=pl.ANY)],
        out_specs=pl.BlockSpec(memory_space=pl.ANY),
        scratch_shapes=[pltpu.SemaphoreType.DMA((len(order),))],
        compiler_params=pltpu.CompilerParams(vmem_limit_bytes=1 << 20),
        cost_estimate=pl.CostEstimate(flops=0, bytes_accessed=2 * features.size * 2, transcendentals=0),
    )(me.astype(jnp.int32)[None], features)


def on_device(features, coeffs, inverse, labels):
    nfeat = lax.axis_size("feat")
    nrows = lax.axis_size("rows")
    block = lax.axis_index("feat")
    me = lax.axis_index("rows")
    own, classes = coeffs.shape
    outer = nrows // INNER
    near = [z * INNER for z in range(outer)]
    quad = [0, 2, 1, 3]
    order = [q + z for q in quad for z in near]

    def picked(array, codes, axis):
        parts = [lax.dynamic_slice_in_dim(array, (me ^ code) * own, own, axis) for code in codes]
        return jnp.concatenate(parts, axis=axis)

    def over_outer(mine):
        return jnp.concatenate([mine] + [swapped(mine, "rows", z) for z in near[1:]], axis=0)

    def over_bit(mine, bit):
        return jnp.concatenate([mine, swapped(mine, "rows", bit)], axis=0)

    coeffs_low = coeffs.astype(LOW)
    blocks = [picked(inverse, [z + q for q in quad], 1).astype(LOW) for z in near]
    inverse_low = jnp.concatenate(
        [blocks[0]] + [swapped(sent, "rows", z) for sent, z in zip(blocks[1:], near[1:])], axis=0
    )
    all_coeffs = over_bit(over_bit(over_outer(coeffs_low), 2), 1)
    features = reordered(features, me, order, own)
    all_coeffs, inverse_low = tied(all_coeffs, inverse_low)

    fitted = jnp.dot(features, all_coeffs, preferred_element_type=WIDE)
    bits = [1 << k for k in range((nfeat - 1).bit_length())]
    for bit in bits[:-1]:
        fitted = fitted + swapped(fitted, "feat", bit)
    fit_high, rest = split(fitted)
    targets = (labels[:, None] == jnp.arange(classes, dtype=jnp.int32)[None, :]).astype(WIDE)
    incoming = (targets - fitted) - swapped(fit_high, "feat", bits[-1]).astype(WIDE)
    incoming_low = incoming.astype(LOW)
    sign = -1.0

    def moved(rest):
        return swapped(rest, "feat", bits[-1])

    contract = (((0,), (0,)), ((), ()))
    kept = jnp.zeros_like(incoming)
    delta_kept = jnp.zeros_like(coeffs)
    for turn in range(nfeat):
        grad = lax.dot_general(features, incoming_low, contract, preferred_element_type=WIDE)
        keep, send = halved(grad)
        grad = keep + swapped(send, "rows", 1)
        keep, send = halved(grad)
        grad = keep + swapped(send.astype(LOW), "rows", 2).astype(WIDE)
        grad_low, rest = tied(grad.astype(LOW), rest)
        parts = [swapped(grad_low, "rows", z) for z in near[1:]]
        *parts, rest = tied(*parts, moved(rest))
        incoming = incoming + sign * rest.astype(WIDE)
        for step, got in enumerate(parts, 1):
            got = got.astype(WIDE)
            grad = grad + jnp.concatenate(
                [got[(slot ^ step) * own:((slot ^ step) + 1) * own] for slot in range(outer)], axis=0
            )
        pair = jnp.concatenate(split(grad), axis=1)
        part = lax.dot_general(inverse_low, pair, contract, preferred_element_type=WIDE)
        part = part[:, :classes] + part[:, classes:]
        keep, send = halved(part)
        part = keep + swapped(send, "rows", 1)
        top, bottom = halved(part)
        delta = part + swapped(jnp.concatenate([bottom, top]).astype(LOW), "rows", 2).astype(WIDE)
        delta_low = delta.astype(LOW)
        slots = [delta_low] + [swapped(delta_low, "rows", z) for z in near[1:]]
        delta_low = jnp.concatenate([s[:own] for s in slots] + [s[own:] for s in slots], axis=0)
        delta_low = over_bit(delta_low, 1)
        outgoing = incoming - jnp.dot(features, delta_low, preferred_element_type=WIDE)
        active = block == turn
        kept = jnp.where(active, outgoing, kept)
        delta_kept = jnp.where(active, delta[:own], delta_kept)
        if turn < nfeat - 1:
            along = [(i, (i + 1) % nfeat) for i in range(nfeat)]
            high, rest = split(outgoing)
            incoming_low = lax.ppermute(high, "feat", along)
            incoming, sign = incoming_low.astype(WIDE), 1.0

            def moved(rest):
                return lax.ppermute(rest, "feat", along)

    squares = jnp.sum(kept * kept, axis=0, keepdims=True)
    squares = lax.all_to_all(
        jnp.broadcast_to(squares[None], (nrows, 1, classes)), "rows", 0, 0, tiled=True
    )
    return (coeffs + delta_kept, kept[None], jnp.sum(squares, axis=0))


def solution(mesh):
    placed = (P("rows", "feat"), P(("feat", "rows"), None), P(("feat", "rows"), None), P("rows"))
    return jax.shard_map(
        on_device,
        mesh=mesh,
        in_specs=placed,
        out_specs=(P(("feat", "rows"), None), P("feat", "rows", None), P("feat", None)),
        check_vma=False,
    )
```

```python
import functools

import jax
import jax.numpy as jnp
from jax import lax
from jax.experimental import pallas as pl
from jax.experimental.pallas import tpu as pltpu
from jax.sharding import PartitionSpec as P

LOW = jnp.bfloat16
WIDE = jnp.float32
INNER = 4


def swapped(shard, axis, bit):
    peers = lax.axis_size(axis)
    return lax.ppermute(shard, axis, [(i, i ^ bit) for i in range(peers)])


def split(wide):
    high = lax.reduce_precision(wide, 8, 7)
    return high.astype(LOW), (wide - high).astype(LOW)


def tied(*arrays):
    return lax.optimization_barrier(arrays)


def halved(whole):
    half = whole.shape[0] // 2
    return whole[:half], whole[half:]


def reorder_kernel(order, own, me_ref, given, taken, sems):
    me = me_ref[0]
    copies = []
    for slot, code in enumerate(order):
        start = pl.multiple_of((me ^ code) * own, own)
        copies.append(
            pltpu.make_async_copy(
                given.at[:, pl.ds(start, own)], taken.at[:, pl.ds(slot * own, own)], sems.at[slot]
            )
        )
    for copy in copies:
        copy.start()
    for copy in copies:
        copy.wait()


def reordered(features, me, order, own):
    if own % 128:
        parts = [lax.dynamic_slice_in_dim(features, (me ^ code) * own, own, 1) for code in order]
        return jnp.concatenate(parts, axis=1)
    return pl.pallas_call(
        functools.partial(reorder_kernel, order, own),
        out_shape=jax.ShapeDtypeStruct(features.shape, features.dtype),
        in_specs=[pl.BlockSpec(memory_space=pltpu.SMEM), pl.BlockSpec(memory_space=pl.ANY)],
        out_specs=pl.BlockSpec(memory_space=pl.ANY),
        scratch_shapes=[pltpu.SemaphoreType.DMA((len(order),))],
        compiler_params=pltpu.CompilerParams(vmem_limit_bytes=1 << 20),
        cost_estimate=pl.CostEstimate(flops=0, bytes_accessed=2 * features.size * 2, transcendentals=0),
    )(me.astype(jnp.int32)[None], features)


def on_device(features, coeffs, inverse, labels):
    nfeat = lax.axis_size("feat")
    nrows = lax.axis_size("rows")
    block = lax.axis_index("feat")
    me = lax.axis_index("rows")
    own, classes = coeffs.shape
    outer = nrows // INNER
    near = [z * INNER for z in range(outer)]
    quad = [0, 2, 1, 3]
    order = [q + z for q in quad for z in near]

    def picked(array, codes, axis):
        parts = [lax.dynamic_slice_in_dim(array, (me ^ code) * own, own, axis) for code in codes]
        return jnp.concatenate(parts, axis=axis)

    def over_outer(mine):
        return jnp.concatenate([mine] + [swapped(mine, "rows", z) for z in near[1:]], axis=0)

    def over_bit(mine, bit):
        return jnp.concatenate([mine, swapped(mine, "rows", bit)], axis=0)

    coeffs_low, *actives = tied(coeffs.astype(LOW), *[block == turn for turn in range(nfeat)])
    blocks = [picked(inverse, [z + q for q in quad], 1).astype(LOW) for z in near]
    near_coeffs, features = tied(over_outer(coeffs_low), reordered(features, me, order, own))
    all_coeffs = over_bit(over_bit(near_coeffs, 2), 1)

    inverse_low = jnp.concatenate(
        [blocks[0]] + [swapped(sent, "rows", z) for sent, z in zip(blocks[1:], near[1:])], axis=0
    )
    fitted = jnp.dot(features, all_coeffs, preferred_element_type=WIDE)
    targets = (labels[:, None] == jnp.arange(classes, dtype=jnp.int32)[None, :]).astype(WIDE)
    if nfeat == 2:
        fit_high, fit_rest = split(fitted)
        fit_high, inverse_low = tied(swapped(fit_high, "feat", 1), inverse_low)
        incoming = (targets - fitted) - fit_high.astype(WIDE)
    else:
        for bit in [1 << k for k in range((nfeat - 1).bit_length())]:
            fitted = fitted + swapped(fitted, "feat", bit)
        incoming = targets - fitted
    incoming_low = incoming.astype(LOW)

    contract = (((0,), (0,)), ((), ()))
    along = [(i, (i + 1) % nfeat) for i in range(nfeat)]
    rest = None
    kept = jnp.zeros_like(incoming)
    delta_kept = jnp.zeros_like(coeffs)
    for turn in range(nfeat):
        grad = lax.dot_general(features, incoming_low, contract, preferred_element_type=WIDE)
        keep, send = halved(grad)
        grad = keep + swapped(send, "rows", 1)
        keep, send = halved(grad)
        got = swapped(send.astype(LOW), "rows", 2)
        grad = keep + got.astype(WIDE)
        grad_low = grad.astype(LOW)
        if turn > 0:
            grad_low, rest = tied(grad_low, rest)
        parts = [swapped(grad_low, "rows", z) for z in near[1:]]
        if turn > 0:
            *parts, rest = tied(*parts, lax.ppermute(rest, "feat", along))
            incoming = incoming + rest.astype(WIDE)
        for step, got in enumerate(parts, 1):
            got = got.astype(WIDE)
            grad = grad + jnp.concatenate(
                [got[(slot ^ step) * own:((slot ^ step) + 1) * own] for slot in range(outer)], axis=0
            )
        pair = jnp.concatenate(split(grad), axis=1)
        part = lax.dot_general(inverse_low, pair, contract, preferred_element_type=WIDE)
        part = part[:, :classes] + part[:, classes:]
        keep, send = halved(part)
        part = keep + swapped(send, "rows", 1)
        top, bottom = halved(part)
        delta = part + swapped(jnp.concatenate([bottom, top]).astype(LOW), "rows", 2).astype(WIDE)
        delta_low = delta.astype(LOW)
        slots = [delta_low] + [swapped(delta_low, "rows", z) for z in near[1:]]
        delta_low = jnp.concatenate([s[:own] for s in slots] + [s[own:] for s in slots], axis=0)
        delta_low = over_bit(delta_low, 1)
        outgoing = incoming - jnp.dot(features, delta_low, preferred_element_type=WIDE)
        active = actives[turn]
        delta_kept = jnp.where(active, delta[:own], delta_kept)
        if turn < nfeat - 1:
            high, rest = split(outgoing)
            if nfeat == 2:
                high = jnp.where(actives[0], high, fit_rest)
            incoming_low = lax.ppermute(high, "feat", along)
            incoming = incoming_low.astype(WIDE)
            if nfeat == 2:
                outgoing = outgoing - incoming
                incoming = incoming - fit_rest.astype(WIDE)
        else:
            outgoing = lax.optimization_barrier(outgoing)
        kept = jnp.where(active, outgoing, kept)

    squares = jnp.sum(kept * kept, axis=0, keepdims=True)
    squares = lax.all_to_all(
        jnp.broadcast_to(squares[None], (nrows, 1, classes)), "rows", 0, 0, tiled=True
    )
    return (coeffs + delta_kept, kept[None], jnp.sum(squares, axis=0))


def solution(mesh):
    placed = (P("rows", "feat"), P(("feat", "rows"), None), P(("feat", "rows"), None), P("rows"))
    return jax.shard_map(
        on_device,
        mesh=mesh,
        in_specs=placed,
        out_specs=(P(("feat", "rows"), None), P("feat", "rows", None), P("feat", None)),
        check_vma=False,
    )
```

```python
import functools

import jax
import jax.numpy as jnp
from jax import lax
from jax.experimental import pallas as pl
from jax.experimental.pallas import tpu as pltpu
from jax.sharding import PartitionSpec as P

LOW = jnp.bfloat16
WIDE = jnp.float32
INNER = 4


def swapped(shard, axis, bit):
    peers = lax.axis_size(axis)
    return lax.ppermute(shard, axis, [(i, i ^ bit) for i in range(peers)])


def split(wide):
    high = lax.reduce_precision(wide, 8, 7)
    return high.astype(LOW), (wide - high).astype(LOW)


def tied(*arrays):
    return lax.optimization_barrier(arrays)


def halved(whole):
    half = whole.shape[0] // 2
    return whole[:half], whole[half:]


def reorder_kernel(order, own, me_ref, given, near, far, sems):
    me = me_ref[0]
    half = len(order) // 2
    copies = []
    for slot, code in enumerate(order):
        start = pl.multiple_of((me ^ code) * own, own)
        place = pl.ds(slot % half * own, own)
        taken = (near if slot < half else far).at[:, place]
        copies.append(pltpu.make_async_copy(given.at[:, pl.ds(start, own)], taken, sems.at[slot]))
    for copy in copies:
        copy.start()
    for copy in copies:
        copy.wait()


def reordered(features, me, order, own):
    samples, width = features.shape
    half = width // 2
    if own % 128:
        column = jnp.arange(width)
        source = (me ^ jnp.repeat(jnp.array(order), own)) * own + column % own
        pick = (column[:, None] == source[None, :]).astype(LOW)
        taken = jnp.dot(features, pick, preferred_element_type=WIDE).astype(LOW)
        return taken[:, :half], taken[:, half:]
    return pl.pallas_call(
        functools.partial(reorder_kernel, order, own),
        out_shape=[jax.ShapeDtypeStruct((samples, half), features.dtype)] * 2,
        in_specs=[pl.BlockSpec(memory_space=pltpu.SMEM), pl.BlockSpec(memory_space=pl.ANY)],
        out_specs=[pl.BlockSpec(memory_space=pl.ANY)] * 2,
        scratch_shapes=[pltpu.SemaphoreType.DMA((len(order),))],
        compiler_params=pltpu.CompilerParams(vmem_limit_bytes=1 << 20),
        cost_estimate=pl.CostEstimate(flops=0, bytes_accessed=2 * features.size * 2, transcendentals=0),
    )(me.astype(jnp.int32)[None], features)


def on_device(features, coeffs, inverse, labels):
    nfeat = lax.axis_size("feat")
    nrows = lax.axis_size("rows")
    block = lax.axis_index("feat")
    me = lax.axis_index("rows")
    own, classes = coeffs.shape
    outer = nrows // INNER
    near = [z * INNER for z in range(outer)]
    quad = [0, 2, 1, 3]
    order = [q + z for q in quad for z in near]

    def picked(array, codes, axis):
        parts = [lax.dynamic_slice_in_dim(array, (me ^ code) * own, own, axis) for code in codes]
        return jnp.concatenate(parts, axis=axis)

    def over_outer(mine):
        return jnp.concatenate([mine] + [swapped(mine, "rows", z) for z in near[1:]], axis=0)

    def over_bit(mine, bit):
        return jnp.concatenate([mine, swapped(mine, "rows", bit)], axis=0)

    coeffs_low, *actives = tied(coeffs.astype(LOW), *[block == turn for turn in range(nfeat)])
    blocks = [picked(inverse, [z + q for q in quad], 1).astype(LOW) for z in near]
    near_coeffs, keeping, sending = tied(over_outer(coeffs_low), *reordered(features, me, order, own))
    near_coeffs = over_bit(near_coeffs, 2)

    def product(rows):
        far = swapped(rows, "rows", 1)
        first, far = tied(jnp.dot(keeping, rows, preferred_element_type=WIDE), far)
        return first + jnp.dot(sending, far, preferred_element_type=WIDE)


    keeping, sending = reordered(features, me, order, own)
    near_coeffs, keeping, *blocks = tied(over_outer(coeffs_low), keeping, *blocks)
    near_coeffs = over_bit(near_coeffs, 2)

    def product(rows):
        far = swapped(rows, "rows", 1)
        first, far = tied(jnp.dot(keeping, rows, preferred_element_type=WIDE), far)
        return first + jnp.dot(sending, far, preferred_element_type=WIDE)


    inverse_low = jnp.concatenate(
        [blocks[0]] + [swapped(sent, "rows", z) for sent, z in zip(blocks[1:], near[1:])], axis=0
    )
    fitted = product(near_coeffs)
    targets = (labels[:, None] == jnp.arange(classes, dtype=jnp.int32)[None, :]).astype(WIDE)
    if nfeat == 2:
        fit_high, fit_rest = split(fitted)
        fit_high, inverse_low = tied(swapped(fit_high, "feat", 1), inverse_low)
        incoming = (targets - fitted) - fit_high.astype(WIDE)
    else:
        for bit in [1 << k for k in range((nfeat - 1).bit_length())]:
            fitted = fitted + swapped(fitted, "feat", bit)
        incoming = targets - fitted
    incoming_low = incoming.astype(LOW)

    contract = (((0,), (0,)), ((), ()))
    along = [(i, (i + 1) % nfeat) for i in range(nfeat)]
    rest = None
    kept = jnp.zeros_like(incoming)
    delta_kept = jnp.zeros_like(coeffs)
    for turn in range(nfeat):
        send = lax.dot_general(sending, incoming_low, contract, preferred_element_type=WIDE)
        grad = lax.dot_general(keeping, incoming_low, contract, preferred_element_type=WIDE)
        grad, got = tied(grad, swapped(send, "rows", 1))
        grad = grad + got
        keep, send = halved(grad)
        got = swapped(send.astype(LOW), "rows", 2)
        grad = keep + got.astype(WIDE)
        grad_low = grad.astype(LOW)
        if turn > 0:
            grad_low, rest = tied(grad_low, rest)
        parts = [swapped(grad_low, "rows", z) for z in near[1:]]
        if turn > 0:
            *parts, rest = tied(*parts, lax.ppermute(rest, "feat", along))
            incoming = incoming + rest.astype(WIDE)
        for step, got in enumerate(parts, 1):
            got = got.astype(WIDE)
            grad = grad + jnp.concatenate(
                [got[(slot ^ step) * own:((slot ^ step) + 1) * own] for slot in range(outer)], axis=0
            )
        pair = jnp.concatenate(split(grad), axis=1)
        part = lax.dot_general(inverse_low, pair, contract, preferred_element_type=WIDE)
        part = part[:, :classes] + part[:, classes:]
        keep, send = halved(part)
        part = keep + swapped(send, "rows", 1)
        top, bottom = halved(part)
        delta = part + swapped(jnp.concatenate([bottom, top]).astype(LOW), "rows", 2).astype(WIDE)
        delta_low = delta.astype(LOW)
        slots = [delta_low] + [swapped(delta_low, "rows", z) for z in near[1:]]
        delta_low = jnp.concatenate([s[:own] for s in slots] + [s[own:] for s in slots], axis=0)
        outgoing = incoming - product(delta_low)
        active = actives[turn]
        delta_kept = jnp.where(active, delta[:own], delta_kept)
        if turn < nfeat - 1:
            high, rest = split(outgoing)
            if nfeat == 2:
                high = jnp.where(actives[0], high, fit_rest)
            incoming_low = lax.ppermute(high, "feat", along)
            incoming = incoming_low.astype(WIDE)
            if nfeat == 2:
                outgoing = outgoing - incoming
                incoming = incoming - fit_rest.astype(WIDE)
        kept = jnp.where(active, outgoing, kept)

    kept = lax.optimization_barrier(kept)
    squares = jnp.sum(kept * kept, axis=0, keepdims=True)
    squares = lax.all_to_all(
        jnp.broadcast_to(squares[None], (nrows, 1, classes)), "rows", 0, 0, tiled=True
    )
    return (coeffs + delta_kept, kept[None], jnp.sum(squares, axis=0))


def solution(mesh):
    placed = (P("rows", "feat"), P(("feat", "rows"), None), P(("feat", "rows"), None), P("rows"))
    return jax.shard_map(
        on_device,
        mesh=mesh,
        in_specs=placed,
        out_specs=(P(("feat", "rows"), None), P("feat", "rows", None), P("feat", None)),
        check_vma=False,
    )
```

```python
import functools

import jax
import jax.numpy as jnp
from jax import lax
from jax.experimental import pallas as pl
from jax.experimental.pallas import tpu as pltpu
from jax.sharding import PartitionSpec as P

LOW = jnp.bfloat16
WIDE = jnp.float32
INNER = 4


def swapped(shard, axis, bit):
    peers = lax.axis_size(axis)
    return lax.ppermute(shard, axis, [(i, i ^ bit) for i in range(peers)])


def split(wide):
    high = lax.reduce_precision(wide, 8, 7)
    return high.astype(LOW), (wide - high).astype(LOW)


def tied(*arrays):
    return lax.optimization_barrier(arrays)


def halved(whole):
    half = whole.shape[0] // 2
    return whole[:half], whole[half:]


def reorder_kernel(order, own, me_ref, given, near, far, sems):
    me = me_ref[0]
    half = len(order) // 2
    copies = []
    for slot, code in enumerate(order):
        start = pl.multiple_of((me ^ code) * own, own)
        place = pl.ds(slot % half * own, own)
        taken = (near if slot < half else far).at[:, place]
        copies.append(pltpu.make_async_copy(given.at[:, pl.ds(start, own)], taken, sems.at[slot]))
    for copy in copies:
        copy.start()
    for copy in copies:
        copy.wait()


def reordered(features, me, order, own):
    samples, width = features.shape
    half = width // 2
    if own % 128:
        column = jnp.arange(width)
        source = (me ^ jnp.repeat(jnp.array(order), own)) * own + column % own
        pick = (column[:, None] == source[None, :]).astype(LOW)
        taken = jnp.dot(features, pick, preferred_element_type=WIDE).astype(LOW)
        return taken[:, :half], taken[:, half:]
    return pl.pallas_call(
        functools.partial(reorder_kernel, order, own),
        out_shape=[jax.ShapeDtypeStruct((samples, half), features.dtype)] * 2,
        in_specs=[pl.BlockSpec(memory_space=pltpu.SMEM), pl.BlockSpec(memory_space=pl.ANY)],
        out_specs=[pl.BlockSpec(memory_space=pl.ANY)] * 2,
        scratch_shapes=[pltpu.SemaphoreType.DMA((len(order),))],
        compiler_params=pltpu.CompilerParams(vmem_limit_bytes=1 << 20),
        cost_estimate=pl.CostEstimate(flops=0, bytes_accessed=2 * features.size * 2, transcendentals=0),
    )(me.astype(jnp.int32)[None], features)


def on_device(features, coeffs, inverse, labels):
    nfeat = lax.axis_size("feat")
    nrows = lax.axis_size("rows")
    block = lax.axis_index("feat")
    me = lax.axis_index("rows")
    own, classes = coeffs.shape
    outer = nrows // INNER
    near = [z * INNER for z in range(outer)]
    quad = [0, 2, 1, 3]
    order = [q + z for q in quad for z in near]

    def picked(array, codes, axis):
        parts = [lax.dynamic_slice_in_dim(array, (me ^ code) * own, own, axis) for code in codes]
        return jnp.concatenate(parts, axis=axis)

    def over_outer(mine):
        return jnp.concatenate([mine] + [swapped(mine, "rows", z) for z in near[1:]], axis=0)

    def over_bit(mine, bit):
        return jnp.concatenate([mine, swapped(mine, "rows", bit)], axis=0)

    coeffs_low, *actives = tied(coeffs.astype(LOW), *[block == turn for turn in range(nfeat)])
    blocks = [picked(inverse, [z + q for q in quad], 1).astype(LOW) for z in near]
    near_coeffs, keeping, sending = tied(over_outer(coeffs_low), *reordered(features, me, order, own))
    near_coeffs = over_bit(near_coeffs, 2)

    def product(rows):
        far = swapped(rows, "rows", 1)
        first, far = tied(jnp.dot(keeping, rows, preferred_element_type=WIDE), far)
        return first + jnp.dot(sending, far, preferred_element_type=WIDE)


    keeping, sending = reordered(features, me, order, own)
    near_coeffs, keeping, *blocks = tied(over_outer(coeffs_low), keeping, *blocks)
    near_coeffs = over_bit(near_coeffs, 2)

    def product(rows):
        far = swapped(rows, "rows", 1)
        first, far = tied(jnp.dot(keeping, rows, preferred_element_type=WIDE), far)
        return first + jnp.dot(sending, far, preferred_element_type=WIDE)


    inverse_low = jnp.concatenate(
        [blocks[0]] + [swapped(sent, "rows", z) for sent, z in zip(blocks[1:], near[1:])], axis=0
    )
    fitted = product(near_coeffs)
    targets = (labels[:, None] == jnp.arange(classes, dtype=jnp.int32)[None, :]).astype(WIDE)
    if nfeat == 2:
        fit_high, fit_rest = split(fitted)
        fit_high, inverse_low = tied(swapped(fit_high, "feat", 1), inverse_low)
        incoming = (targets - fitted) - fit_high.astype(WIDE)
    else:
        for bit in [1 << k for k in range((nfeat - 1).bit_length())]:
            fitted = fitted + swapped(fitted, "feat", bit)
        incoming = targets - fitted
    incoming_low = incoming.astype(LOW)

    contract = (((0,), (0,)), ((), ()))
    along = [(i, (i + 1) % nfeat) for i in range(nfeat)]
    rest = None
    kept = jnp.zeros_like(incoming)
    delta_kept = jnp.zeros_like(coeffs)
    for turn in range(nfeat):
        send = lax.dot_general(sending, incoming_low, contract, preferred_element_type=WIDE)
        grad = lax.dot_general(keeping, incoming_low, contract, preferred_element_type=WIDE)
        grad, got = tied(grad, swapped(send, "rows", 1))
        grad = grad + got
        keep, send = halved(grad)
        got = swapped(send.astype(LOW), "rows", 2)
        grad = keep + got.astype(WIDE)
        grad_low = grad.astype(LOW)
        if turn > 0 and nfeat > 2:
            grad_low, rest = tied(grad_low, rest)
        parts = [swapped(grad_low, "rows", z) for z in near[1:]]
        if turn > 0 and nfeat > 2:
            *parts, rest = tied(*parts, lax.ppermute(rest, "feat", along))
            incoming = incoming + rest.astype(WIDE)
        for step, got in enumerate(parts, 1):
            got = got.astype(WIDE)
            grad = grad + jnp.concatenate(
                [got[(slot ^ step) * own:((slot ^ step) + 1) * own] for slot in range(outer)], axis=0
            )
        pair = jnp.concatenate(split(grad), axis=1)
        part = lax.dot_general(inverse_low, pair, contract, preferred_element_type=WIDE)
        part = part[:, :classes] + part[:, classes:]
        keep, send = halved(part)
        part = keep + swapped(send, "rows", 1)
        top, bottom = halved(part)
        delta = part + swapped(jnp.concatenate([bottom, top]).astype(LOW), "rows", 2).astype(WIDE)
        delta_low = delta.astype(LOW)
        slots = [delta_low] + [swapped(delta_low, "rows", z) for z in near[1:]]
        delta_low = jnp.concatenate([s[:own] for s in slots] + [s[own:] for s in slots], axis=0)
        change = product(delta_low)
        outgoing = incoming - change
        active = actives[turn]
        delta_kept = jnp.where(active, delta[:own], delta_kept)
        if turn < nfeat - 1 and nfeat == 2:
            sent = jnp.where(actives[0], change + fit_rest.astype(WIDE), fit_rest.astype(WIDE))
            got = lax.ppermute(sent.astype(LOW), "feat", along).astype(WIDE)
            outgoing = outgoing - got
            incoming = incoming - got
            incoming_low = incoming.astype(LOW)
        elif turn < nfeat - 1:
            high, rest = split(outgoing)
            incoming_low = lax.ppermute(high, "feat", along)
            incoming = incoming_low.astype(WIDE)
        kept = jnp.where(active, outgoing, kept)

    kept = lax.optimization_barrier(kept)
    squares = jnp.sum(kept * kept, axis=0, keepdims=True)
    squares = lax.all_to_all(
        jnp.broadcast_to(squares[None], (nrows, 1, classes)), "rows", 0, 0, tiled=True
    )
    return (coeffs + delta_kept, kept[None], jnp.sum(squares, axis=0))


def solution(mesh):
    placed = (P("rows", "feat"), P(("feat", "rows"), None), P(("feat", "rows"), None), P("rows"))
    return jax.shard_map(
        on_device,
        mesh=mesh,
        in_specs=placed,
        out_specs=(P(("feat", "rows"), None), P("feat", "rows", None), P("feat", None)),
        check_vma=False,
    )
```

```python
import functools

import jax
import jax.numpy as jnp
from jax import lax
from jax.experimental import pallas as pl
from jax.experimental.pallas import tpu as pltpu
from jax.sharding import PartitionSpec as P

LOW = jnp.bfloat16
WIDE = jnp.float32
INNER = 4


def swapped(shard, axis, bit):
    peers = lax.axis_size(axis)
    return lax.ppermute(shard, axis, [(i, i ^ bit) for i in range(peers)])


def split(wide):
    high = lax.reduce_precision(wide, 8, 7)
    return high.astype(LOW), (wide - high).astype(LOW)


def tied(*arrays):
    return lax.optimization_barrier(arrays)


def halved(whole):
    half = whole.shape[0] // 2
    return whole[:half], whole[half:]


def reorder_kernel(order, own, me_ref, given, near, far, sems):
    me = me_ref[0]
    half = len(order) // 2
    copies = []
    for slot, code in enumerate(order):
        start = pl.multiple_of((me ^ code) * own, own)
        place = pl.ds(slot % half * own, own)
        taken = (near if slot < half else far).at[:, place]
        copies.append(pltpu.make_async_copy(given.at[:, pl.ds(start, own)], taken, sems.at[slot]))
    for copy in copies:
        copy.start()
    for copy in copies:
        copy.wait()


def reordered(features, me, order, own):
    samples, width = features.shape
    half = width // 2
    if own % 128:
        column = jnp.arange(width)
        source = (me ^ jnp.repeat(jnp.array(order), own)) * own + column % own
        pick = (column[:, None] == source[None, :]).astype(LOW)
        taken = jnp.dot(features, pick, preferred_element_type=WIDE).astype(LOW)
        return taken[:, :half], taken[:, half:]
    return pl.pallas_call(
        functools.partial(reorder_kernel, order, own),
        out_shape=[jax.ShapeDtypeStruct((samples, half), features.dtype)] * 2,
        in_specs=[pl.BlockSpec(memory_space=pltpu.SMEM), pl.BlockSpec(memory_space=pl.ANY)],
        out_specs=[pl.BlockSpec(memory_space=pl.ANY)] * 2,
        scratch_shapes=[pltpu.SemaphoreType.DMA((len(order),))],
        compiler_params=pltpu.CompilerParams(vmem_limit_bytes=48 << 20),
        cost_estimate=pl.CostEstimate(flops=0, bytes_accessed=2 * features.size * 2, transcendentals=0),
    )(me.astype(jnp.int32)[None], features)


def on_device(features, coeffs, inverse, labels):
    nfeat = lax.axis_size("feat")
    nrows = lax.axis_size("rows")
    block = lax.axis_index("feat")
    me = lax.axis_index("rows")
    own, classes = coeffs.shape
    outer = nrows // INNER
    near = [z * INNER for z in range(outer)]
    quad = [0, 2, 1, 3]
    order = [q + z for q in quad for z in near]

    def picked(array, codes, axis):
        parts = [lax.dynamic_slice_in_dim(array, (me ^ code) * own, own, axis) for code in codes]
        return jnp.concatenate(parts, axis=axis)

    def over_outer(mine):
        return jnp.concatenate([mine] + [swapped(mine, "rows", z) for z in near[1:]], axis=0)

    def over_bit(mine, bit):
        return jnp.concatenate([mine, swapped(mine, "rows", bit)], axis=0)

    coeffs_low, *actives = tied(coeffs.astype(LOW), *[block == turn for turn in range(nfeat)])
    blocks = [picked(inverse, [z + q for q in quad], 1).astype(LOW) for z in near]
    near_coeffs, keeping, sending = tied(over_outer(coeffs_low), *reordered(features, me, order, own))
    near_coeffs = over_bit(near_coeffs, 2)

    def product(rows):
        far = swapped(rows, "rows", 1)
        first, far = tied(jnp.dot(keeping, rows, preferred_element_type=WIDE), far)
        return first + jnp.dot(sending, far, preferred_element_type=WIDE)


    keeping, sending = reordered(features, me, order, own)
    near_coeffs, keeping, *blocks = tied(over_outer(coeffs_low), keeping, *blocks)
    near_coeffs = over_bit(near_coeffs, 2)

    def product(rows):
        far = swapped(rows, "rows", 1)
        first, far = tied(jnp.dot(keeping, rows, preferred_element_type=WIDE), far)
        return first + jnp.dot(sending, far, preferred_element_type=WIDE)


    inverse_low = jnp.concatenate(
        [blocks[0]] + [swapped(sent, "rows", z) for sent, z in zip(blocks[1:], near[1:])], axis=0
    )
    fitted = product(near_coeffs)
    targets = (labels[:, None] == jnp.arange(classes, dtype=jnp.int32)[None, :]).astype(WIDE)
    if nfeat == 2:
        fit_high, fit_rest = split(fitted)
        fit_high, inverse_low = tied(swapped(fit_high, "feat", 1), inverse_low)
        incoming = (targets - fitted) - fit_high.astype(WIDE)
    else:
        for bit in [1 << k for k in range((nfeat - 1).bit_length())]:
            fitted = fitted + swapped(fitted, "feat", bit)
        incoming = targets - fitted
    incoming_low = incoming.astype(LOW)

    contract = (((0,), (0,)), ((), ()))
    along = [(i, (i + 1) % nfeat) for i in range(nfeat)]
    rest = None
    kept = jnp.zeros_like(incoming)
    delta_kept = jnp.zeros_like(coeffs)
    for turn in range(nfeat):
        send = lax.dot_general(sending, incoming_low, contract, preferred_element_type=WIDE)
        grad = lax.dot_general(keeping, incoming_low, contract, preferred_element_type=WIDE)
        grad, got = tied(grad, swapped(send, "rows", 1))
        grad = grad + got
        keep, send = halved(grad)
        got = swapped(send.astype(LOW), "rows", 2)
        grad = keep + got.astype(WIDE)
        grad_low = grad.astype(LOW)
        if turn > 0 and nfeat > 2:
            grad_low, rest = tied(grad_low, rest)
        parts = [swapped(grad_low, "rows", z) for z in near[1:]]
        if turn > 0 and nfeat > 2:
            *parts, rest = tied(*parts, lax.ppermute(rest, "feat", along))
            incoming = incoming + rest.astype(WIDE)
        for step, got in enumerate(parts, 1):
            got = got.astype(WIDE)
            grad = grad + jnp.concatenate(
                [got[(slot ^ step) * own:((slot ^ step) + 1) * own] for slot in range(outer)], axis=0
            )
        pair = jnp.concatenate(split(grad), axis=1)
        part = lax.dot_general(inverse_low, pair, contract, preferred_element_type=WIDE)
        part = part[:, :classes] + part[:, classes:]
        keep, send = halved(part)
        part = keep + swapped(send, "rows", 1)
        top, bottom = halved(part)
        delta = part + swapped(jnp.concatenate([bottom, top]).astype(LOW), "rows", 2).astype(WIDE)
        delta_low = delta.astype(LOW)
        slots = [delta_low] + [swapped(delta_low, "rows", z) for z in near[1:]]
        delta_low = jnp.concatenate([s[:own] for s in slots] + [s[own:] for s in slots], axis=0)
        change = product(delta_low)
        outgoing = incoming - change
        active = actives[turn]
        delta_kept = jnp.where(active, delta[:own], delta_kept)
        if turn < nfeat - 1 and nfeat == 2:
            sent = jnp.where(actives[0], change + fit_rest.astype(WIDE), fit_rest.astype(WIDE))
            got = lax.ppermute(sent.astype(LOW), "feat", along).astype(WIDE)
            outgoing = outgoing - got
            incoming = incoming - got
            incoming_low = incoming.astype(LOW)
        elif turn < nfeat - 1:
            high, rest = split(outgoing)
            incoming_low = lax.ppermute(high, "feat", along)
            incoming = incoming_low.astype(WIDE)
        kept = jnp.where(active, outgoing, kept)

    kept = lax.optimization_barrier(kept)
    squares = jnp.sum(kept * kept, axis=0, keepdims=True)
    squares = lax.all_to_all(
        jnp.broadcast_to(squares[None], (nrows, 1, classes)), "rows", 0, 0, tiled=True
    )
    return (coeffs + delta_kept, kept[None], jnp.sum(squares, axis=0))


def solution(mesh):
    placed = (P("rows", "feat"), P(("feat", "rows"), None), P(("feat", "rows"), None), P("rows"))
    return jax.shard_map(
        on_device,
        mesh=mesh,
        in_specs=placed,
        out_specs=(P(("feat", "rows"), None), P("feat", "rows", None), P("feat", None)),
        check_vma=False,
    )
```

```python
import functools

import jax
import jax.numpy as jnp
from jax import lax
from jax.experimental import pallas as pl
from jax.experimental.pallas import tpu as pltpu
from jax.sharding import PartitionSpec as P

LOW = jnp.bfloat16
WIDE = jnp.float32
INNER = 4


def swapped(shard, axis, bit):
    peers = lax.axis_size(axis)
    return lax.ppermute(shard, axis, [(i, i ^ bit) for i in range(peers)])


def split(wide):
    high = lax.reduce_precision(wide, 8, 7)
    return high.astype(LOW), (wide - high).astype(LOW)


def tied(*arrays):
    return lax.optimization_barrier(arrays)


def halved(whole):
    half = whole.shape[0] // 2
    return whole[:half], whole[half:]


def reorder_kernel(order, own, me_ref, given, near, far, sems):
    me = me_ref[0]
    half = len(order) // 2
    copies = []
    for slot, code in enumerate(order):
        start = pl.multiple_of((me ^ code) * own, own)
        place = pl.ds(slot % half * own, own)
        taken = (near if slot < half else far).at[:, place]
        copies.append(pltpu.make_async_copy(given.at[:, pl.ds(start, own)], taken, sems.at[slot]))
    for copy in copies:
        copy.start()
    for copy in copies:
        copy.wait()


def reordered(features, me, order, own):
    samples, width = features.shape
    half = width // 2
    if own % 128:
        column = jnp.arange(width)
        source = (me ^ jnp.repeat(jnp.array(order), own)) * own + column % own
        pick = (column[:, None] == source[None, :]).astype(LOW)
        taken = jnp.dot(features, pick, preferred_element_type=WIDE).astype(LOW)
        return taken[:, :half], taken[:, half:]
    return pl.pallas_call(
        functools.partial(reorder_kernel, order, own),
        out_shape=[jax.ShapeDtypeStruct((samples, half), features.dtype)] * 2,
        in_specs=[pl.BlockSpec(memory_space=pltpu.SMEM), pl.BlockSpec(memory_space=pl.ANY)],
        out_specs=[pl.BlockSpec(memory_space=pl.ANY)] * 2,
        scratch_shapes=[pltpu.SemaphoreType.DMA((len(order),))],
        compiler_params=pltpu.CompilerParams(vmem_limit_bytes=48 << 20),
        cost_estimate=pl.CostEstimate(flops=0, bytes_accessed=2 * features.size * 2, transcendentals=0),
    )(me.astype(jnp.int32)[None], features)


def on_device(features, coeffs, inverse, labels):
    nfeat = lax.axis_size("feat")
    nrows = lax.axis_size("rows")
    block = lax.axis_index("feat")
    me = lax.axis_index("rows")
    own, classes = coeffs.shape
    outer = nrows // INNER
    near = [z * INNER for z in range(outer)]
    quad = [0, 2, 1, 3]
    order = [q + z for q in quad for z in near]

    def picked(array, codes, axis):
        parts = [lax.dynamic_slice_in_dim(array, (me ^ code) * own, own, axis) for code in codes]
        return jnp.concatenate(parts, axis=axis)

    def over_outer(mine):
        return jnp.concatenate([mine] + [swapped(mine, "rows", z) for z in near[1:]], axis=0)

    def over_bit(mine, bit):
        return jnp.concatenate([mine, swapped(mine, "rows", bit)], axis=0)

    coeffs_low, *actives = tied(coeffs.astype(LOW), *[block == turn for turn in range(nfeat)])
    blocks = [picked(inverse, [z + q for q in quad], 1).astype(LOW) for z in near]
    near_coeffs, keeping, sending = tied(over_outer(coeffs_low), *reordered(features, me, order, own))
    near_coeffs = over_bit(near_coeffs, 2)

    def product(rows):
        far = swapped(rows, "rows", 1)
        first, far = tied(jnp.dot(keeping, rows, preferred_element_type=WIDE), far)
        return first + jnp.dot(sending, far, preferred_element_type=WIDE)


    keeping, sending = reordered(features, me, order, own)
    near_coeffs, keeping, *blocks = tied(over_outer(coeffs_low), keeping, *blocks)
    near_coeffs = over_bit(near_coeffs, 2)

    def product(rows):
        far = swapped(rows, "rows", 1)
        first, far = tied(jnp.dot(keeping, rows, preferred_element_type=WIDE), far)
        return first + jnp.dot(sending, far, preferred_element_type=WIDE)


    inverse_low = jnp.concatenate(
        [blocks[0]] + [swapped(sent, "rows", z) for sent, z in zip(blocks[1:], near[1:])], axis=0
    )
    fitted = product(near_coeffs)
    targets = (labels[:, None] == jnp.arange(classes, dtype=jnp.int32)[None, :]).astype(WIDE)
    if nfeat == 2:
        fit_high, fit_rest = split(fitted)
        fit_high, inverse = tied(fit_high, inverse)
        fit_high, inverse_low = tied(swapped(fit_high, "feat", 1), inverse_low)
        incoming = (targets - fitted) - fit_high.astype(WIDE)
    else:
        for bit in [1 << k for k in range((nfeat - 1).bit_length())]:
            fitted = fitted + swapped(fitted, "feat", bit)
        incoming = targets - fitted
    incoming_low = incoming.astype(LOW)

    own_rest = split(picked(inverse, [z + q for q in quad for z in near[:1]], 1))[1]
    inverse_low = jnp.concatenate([inverse_low, own_rest], axis=0)

    contract = (((0,), (0,)), ((), ()))
    along = [(i, (i + 1) % nfeat) for i in range(nfeat)]
    rest = None
    kept = jnp.zeros_like(incoming)
    delta_kept = jnp.zeros_like(coeffs)
    for turn in range(nfeat):
        send = lax.dot_general(sending, incoming_low, contract, preferred_element_type=WIDE)
        grad = lax.dot_general(keeping, incoming_low, contract, preferred_element_type=WIDE)
        grad, got = tied(grad, swapped(send.astype(LOW), "rows", 1))
        grad = grad + got.astype(WIDE)
        keep, send = halved(grad)
        got = swapped(send.astype(LOW), "rows", 2)
        grad = keep + got.astype(WIDE)
        grad_low = grad.astype(LOW)
        if turn > 0 and nfeat > 2:
            grad_low, rest = tied(grad_low, rest)
        parts = [swapped(grad_low, "rows", z) for z in near[1:]]
        if turn > 0 and nfeat > 2:
            *parts, rest = tied(*parts, lax.ppermute(rest, "feat", along))
            incoming = incoming + rest.astype(WIDE)
        for step, got in enumerate(parts, 1):
            got = got.astype(WIDE)
            grad = grad + jnp.concatenate(
                [got[(slot ^ step) * own:((slot ^ step) + 1) * own] for slot in range(outer)], axis=0
            )
        pair = jnp.concatenate(split(jnp.concatenate([grad, grad[:own]], axis=0)), axis=1)
        part = lax.dot_general(inverse_low, pair, contract, preferred_element_type=WIDE)
        part = part[:, :classes] + part[:, classes:]
        keep, send = halved(part)
        part = keep + swapped(send, "rows", 1)
        top, bottom = halved(part)
        delta = part + swapped(jnp.concatenate([bottom, top]).astype(LOW), "rows", 2).astype(WIDE)
        delta_low = delta.astype(LOW)
        slots = [delta_low] + [swapped(delta_low, "rows", z) for z in near[1:]]
        delta_low = jnp.concatenate([s[:own] for s in slots] + [s[own:] for s in slots], axis=0)
        change = product(delta_low)
        outgoing = incoming - change
        active = actives[turn]
        delta_kept = jnp.where(active, delta[:own], delta_kept)
        if turn < nfeat - 1 and nfeat == 2:
            sent = jnp.where(actives[0], change + fit_rest.astype(WIDE), fit_rest.astype(WIDE))
            got = lax.ppermute(sent.astype(LOW), "feat", along).astype(WIDE)
            outgoing = outgoing - got
            incoming = incoming - got
            incoming_low = incoming.astype(LOW)
        elif turn < nfeat - 1:
            high, rest = split(outgoing)
            incoming_low = lax.ppermute(high, "feat", along)
            incoming = incoming_low.astype(WIDE)
        kept = jnp.where(active, outgoing, kept)

    kept = lax.optimization_barrier(kept)
    squares = jnp.sum(kept * kept, axis=0, keepdims=True)
    squares = lax.all_to_all(
        jnp.broadcast_to(squares[None], (nrows, 1, classes)), "rows", 0, 0, tiled=True
    )
    return (coeffs + delta_kept, kept[None], jnp.sum(squares, axis=0))


def solution(mesh):
    placed = (P("rows", "feat"), P(("feat", "rows"), None), P(("feat", "rows"), None), P("rows"))
    return jax.shard_map(
        on_device,
        mesh=mesh,
        in_specs=placed,
        out_specs=(P(("feat", "rows"), None), P("feat", "rows", None), P("feat", None)),
        check_vma=False,
    )
```

```python
import functools

import jax
import jax.numpy as jnp
from jax import lax
from jax.experimental import pallas as pl
from jax.experimental.pallas import tpu as pltpu
from jax.sharding import PartitionSpec as P

LOW = jnp.bfloat16
WIDE = jnp.float32
INNER = 4


def swapped(shard, axis, bit):
    peers = lax.axis_size(axis)
    return lax.ppermute(shard, axis, [(i, i ^ bit) for i in range(peers)])


def split(wide):
    high = lax.reduce_precision(wide, 8, 7)
    return high.astype(LOW), (wide - high).astype(LOW)


def tied(*arrays):
    return lax.optimization_barrier(arrays)


def halved(whole):
    half = whole.shape[0] // 2
    return whole[:half], whole[half:]


def reorder_kernel(order, own, me_ref, given, near, far, sems):
    me = me_ref[0]
    half = len(order) // 2
    copies = []
    for slot, code in enumerate(order):
        start = pl.multiple_of((me ^ code) * own, own)
        place = pl.ds(slot % half * own, own)
        taken = (near if slot < half else far).at[:, place]
        copies.append(pltpu.make_async_copy(given.at[:, pl.ds(start, own)], taken, sems.at[slot]))
    for copy in copies:
        copy.start()
    for copy in copies:
        copy.wait()


def reordered(features, me, order, own):
    samples, width = features.shape
    half = width // 2
    if own % 128:
        column = jnp.arange(width)
        source = (me ^ jnp.repeat(jnp.array(order), own)) * own + column % own
        pick = (column[:, None] == source[None, :]).astype(LOW)
        taken = jnp.dot(features, pick, preferred_element_type=WIDE).astype(LOW)
        return taken[:, :half], taken[:, half:]
    return pl.pallas_call(
        functools.partial(reorder_kernel, order, own),
        out_shape=[jax.ShapeDtypeStruct((samples, half), features.dtype)] * 2,
        in_specs=[pl.BlockSpec(memory_space=pltpu.SMEM), pl.BlockSpec(memory_space=pl.ANY)],
        out_specs=[pl.BlockSpec(memory_space=pl.ANY)] * 2,
        scratch_shapes=[pltpu.SemaphoreType.DMA((len(order),))],
        compiler_params=pltpu.CompilerParams(vmem_limit_bytes=48 << 20),
        cost_estimate=pl.CostEstimate(flops=0, bytes_accessed=2 * features.size * 2, transcendentals=0),
    )(me.astype(jnp.int32)[None], features)


def on_device(features, coeffs, inverse, labels):
    nfeat = lax.axis_size("feat")
    nrows = lax.axis_size("rows")
    block = lax.axis_index("feat")
    me = lax.axis_index("rows")
    own, classes = coeffs.shape
    outer = nrows // INNER
    near = [z * INNER for z in range(outer)]
    quad = [0, 2, 1, 3]
    order = [q + z for q in quad for z in near]

    def picked(array, codes, axis):
        parts = [lax.dynamic_slice_in_dim(array, (me ^ code) * own, own, axis) for code in codes]
        return jnp.concatenate(parts, axis=axis)

    def over_outer(mine):
        return jnp.concatenate([mine] + [swapped(mine, "rows", z) for z in near[1:]], axis=0)

    def over_bit(mine, bit):
        return jnp.concatenate([mine, swapped(mine, "rows", bit)], axis=0)

    wide_coeffs, *actives = tied(coeffs, *[block == turn for turn in range(nfeat)])
    blocks = [picked(inverse, [z + q for q in quad], 1).astype(LOW) for z in near]

    def product(rows):
        far = swapped(rows, "rows", 1)
        first, far = tied(jnp.dot(keeping, rows, preferred_element_type=WIDE), far)
        return first + jnp.dot(sending, far, preferred_element_type=WIDE)


    keeping, sending = reordered(features, me, order, own)
    near_coeffs, keeping, *blocks = tied(over_outer(wide_coeffs), keeping, *blocks)
    near_coeffs = over_bit(near_coeffs.astype(LOW), 2)

    def product(rows):
        far = swapped(rows, "rows", 1)
        first, far = tied(jnp.dot(keeping, rows, preferred_element_type=WIDE), far)
        return first + jnp.dot(sending, far, preferred_element_type=WIDE)


    inverse_low = jnp.concatenate(
        [blocks[0]] + [swapped(sent, "rows", z) for sent, z in zip(blocks[1:], near[1:])], axis=0
    )
    fitted = product(near_coeffs)
    targets = (labels[:, None] == jnp.arange(classes, dtype=jnp.int32)[None, :]).astype(WIDE)
    if nfeat == 2:
        fit_high, fit_rest = split(fitted)
        fit_high, inverse = tied(fit_high, inverse)
        fit_high, inverse_low = tied(swapped(fit_high, "feat", 1), inverse_low)
        incoming = (targets - fitted) - fit_high.astype(WIDE)
    else:
        for bit in [1 << k for k in range((nfeat - 1).bit_length())]:
            fitted = fitted + swapped(fitted, "feat", bit)
        incoming = targets - fitted
    incoming_low = incoming.astype(LOW)

    own_rest = split(picked(inverse, [z + q for q in quad for z in near[:1]], 1))[1]
    inverse_low = jnp.concatenate([inverse_low, own_rest], axis=0)

    contract = (((0,), (0,)), ((), ()))
    along = [(i, (i + 1) % nfeat) for i in range(nfeat)]
    rest = None
    kept = jnp.zeros_like(incoming)
    delta_kept = jnp.zeros_like(coeffs)
    for turn in range(nfeat):
        send = lax.dot_general(sending, incoming_low, contract, preferred_element_type=WIDE)
        grad = lax.dot_general(keeping, incoming_low, contract, preferred_element_type=WIDE)
        grad, got = tied(grad, swapped(send.astype(LOW), "rows", 1))
        grad = grad + got.astype(WIDE)
        keep, send = halved(grad)
        got = swapped(send.astype(LOW), "rows", 2)
        grad = keep + got.astype(WIDE)
        grad_low = grad.astype(LOW)
        if turn > 0 and nfeat > 2:
            grad_low, rest = tied(grad_low, rest)
        parts = [swapped(grad_low, "rows", z) for z in near[1:]]
        if turn > 0 and nfeat > 2:
            *parts, rest = tied(*parts, lax.ppermute(rest, "feat", along))
            incoming = incoming + rest.astype(WIDE)
        for step, got in enumerate(parts, 1):
            got = got.astype(WIDE)
            grad = grad + jnp.concatenate(
                [got[(slot ^ step) * own:((slot ^ step) + 1) * own] for slot in range(outer)], axis=0
            )
        pair = jnp.concatenate(split(jnp.concatenate([grad, grad[:own]], axis=0)), axis=1)
        part = lax.dot_general(inverse_low, pair, contract, preferred_element_type=WIDE)
        part = part[:, :classes] + part[:, classes:]
        keep, send = halved(part)
        part = keep + swapped(send, "rows", 1)
        top, bottom = halved(part)
        delta = part + swapped(jnp.concatenate([bottom, top]).astype(LOW), "rows", 2).astype(WIDE)
        delta_low = delta.astype(LOW)
        slots = [delta_low] + [swapped(delta_low, "rows", z) for z in near[1:]]
        delta_low = jnp.concatenate([s[:own] for s in slots] + [s[own:] for s in slots], axis=0)
        change = product(delta_low)
        outgoing = incoming - change
        active = actives[turn]
        delta_kept = jnp.where(active, delta[:own], delta_kept)
        if turn < nfeat - 1 and nfeat == 2:
            sent = jnp.where(actives[0], change + fit_rest.astype(WIDE), fit_rest.astype(WIDE))
            got = lax.ppermute(sent.astype(LOW), "feat", along).astype(WIDE)
            outgoing = outgoing - got
            incoming = incoming - got
            incoming_low = incoming.astype(LOW)
        elif turn < nfeat - 1:
            high, rest = split(outgoing)
            incoming_low = lax.ppermute(high, "feat", along)
            incoming = incoming_low.astype(WIDE)
        kept = jnp.where(active, outgoing, kept)

    kept = lax.optimization_barrier(kept)
    squares = jnp.sum(kept * kept, axis=0, keepdims=True)
    squares = lax.all_to_all(
        jnp.broadcast_to(squares[None], (nrows, 1, classes)), "rows", 0, 0, tiled=True
    )
    return (coeffs + delta_kept, kept[None], jnp.sum(squares, axis=0))


def solution(mesh):
    placed = (P("rows", "feat"), P(("feat", "rows"), None), P(("feat", "rows"), None), P("rows"))
    return jax.shard_map(
        on_device,
        mesh=mesh,
        in_specs=placed,
        out_specs=(P(("feat", "rows"), None), P("feat", "rows", None), P("feat", None)),
        check_vma=False,
    )
```

```python
import functools

import jax
import jax.numpy as jnp
from jax import lax
from jax.experimental import pallas as pl
from jax.experimental.pallas import tpu as pltpu
from jax.sharding import PartitionSpec as P

LOW = jnp.bfloat16
WIDE = jnp.float32
INNER = 4


def swapped(shard, axis, bit):
    peers = lax.axis_size(axis)
    return lax.ppermute(shard, axis, [(i, i ^ bit) for i in range(peers)])


def split(wide):
    high = lax.reduce_precision(wide, 8, 7)
    return high.astype(LOW), (wide - high).astype(LOW)


def tied(*arrays):
    return lax.optimization_barrier(arrays)


def halved(whole):
    half = whole.shape[0] // 2
    return whole[:half], whole[half:]


def reorder_kernel(order, own, me_ref, given, near, far, sems):
    me = me_ref[0]
    half = len(order) // 2
    copies = []
    for slot, code in enumerate(order):
        start = pl.multiple_of((me ^ code) * own, own)
        place = pl.ds(slot % half * own, own)
        taken = (near if slot < half else far).at[:, place]
        copies.append(pltpu.make_async_copy(given.at[:, pl.ds(start, own)], taken, sems.at[slot]))
    for copy in copies:
        copy.start()
    for copy in copies:
        copy.wait()


def reordered(features, me, order, own):
    samples, width = features.shape
    half = width // 2
    if own % 128:
        column = jnp.arange(width)
        source = (me ^ jnp.repeat(jnp.array(order), own)) * own + column % own
        pick = (column[:, None] == source[None, :]).astype(LOW)
        taken = jnp.dot(features, pick, preferred_element_type=WIDE).astype(LOW)
        return taken[:, :half], taken[:, half:]
    return pl.pallas_call(
        functools.partial(reorder_kernel, order, own),
        out_shape=[jax.ShapeDtypeStruct((samples, half), features.dtype)] * 2,
        in_specs=[pl.BlockSpec(memory_space=pltpu.SMEM), pl.BlockSpec(memory_space=pl.ANY)],
        out_specs=[pl.BlockSpec(memory_space=pl.ANY)] * 2,
        scratch_shapes=[pltpu.SemaphoreType.DMA((len(order),))],
        compiler_params=pltpu.CompilerParams(vmem_limit_bytes=48 << 20),
        cost_estimate=pl.CostEstimate(flops=0, bytes_accessed=2 * features.size * 2, transcendentals=0),
    )(me.astype(jnp.int32)[None], features)


def on_device(features, coeffs, inverse, labels):
    nfeat = lax.axis_size("feat")
    nrows = lax.axis_size("rows")
    block = lax.axis_index("feat")
    me = lax.axis_index("rows")
    own, classes = coeffs.shape
    outer = nrows // INNER
    near = [z * INNER for z in range(outer)]
    quad = [0, 2, 1, 3]
    order = [q + z for q in quad for z in near]

    def picked(array, codes, axis):
        parts = [lax.dynamic_slice_in_dim(array, (me ^ code) * own, own, axis) for code in codes]
        return jnp.concatenate(parts, axis=axis)

    def over_outer(mine):
        return jnp.concatenate([mine] + [swapped(mine, "rows", z) for z in near[1:]], axis=0)

    def over_bit(mine, bit):
        return jnp.concatenate([mine, swapped(mine, "rows", bit)], axis=0)

    wide_coeffs, *actives = tied(coeffs, *[block == turn for turn in range(nfeat)])
    blocks = [picked(inverse, [z + q for q in quad], 1).astype(LOW) for z in near]

    def product(rows):
        far = swapped(rows, "rows", 1)
        first, far = tied(jnp.dot(keeping, rows, preferred_element_type=WIDE), far)
        return first + jnp.dot(sending, far, preferred_element_type=WIDE)


    keeping, sending = reordered(features, me, order, own)
    near_coeffs, keeping, *blocks = tied(over_outer(wide_coeffs), keeping, *blocks)
    near_coeffs = over_bit(near_coeffs.astype(LOW), 2)

    def product(rows):
        far = swapped(rows, "rows", 1)
        first, far = tied(jnp.dot(keeping, rows, preferred_element_type=WIDE), far)
        return first + jnp.dot(sending, far, preferred_element_type=WIDE)


    inverse_low = jnp.concatenate(
        [blocks[0]] + [swapped(sent, "rows", z) for sent, z in zip(blocks[1:], near[1:])], axis=0
    )
    fitted = product(near_coeffs)
    targets = (labels[:, None] == jnp.arange(classes, dtype=jnp.int32)[None, :]).astype(WIDE)
    if nfeat == 2:
        fit_high, fit_rest = split(fitted)
        fit_high, inverse = tied(fit_high, inverse)
        fit_high, inverse_low = tied(swapped(fit_high, "feat", 1), inverse_low)
        incoming = (targets - fitted) - fit_high.astype(WIDE)
    else:
        for bit in [1 << k for k in range((nfeat - 1).bit_length())]:
            fitted = fitted + swapped(fitted, "feat", bit)
        incoming = targets - fitted
    incoming_low = incoming.astype(LOW)

    own_rest = split(picked(inverse, [z + q for q in quad for z in near[:1]], 1))[1]
    inverse_low = jnp.concatenate([inverse_low, own_rest], axis=0)

    contract = (((0,), (0,)), ((), ()))
    along = [(i, (i + 1) % nfeat) for i in range(nfeat)]
    rest = None
    kept = jnp.zeros_like(incoming)
    delta_kept = jnp.zeros_like(coeffs)
    for turn in range(nfeat):
        send = lax.dot_general(sending, incoming_low, contract, preferred_element_type=WIDE)
        grad = lax.dot_general(keeping, incoming_low, contract, preferred_element_type=WIDE)
        grad, got = tied(grad, swapped(send.astype(LOW), "rows", 1))
        grad = grad + got.astype(WIDE)
        keep, send = halved(grad)
        got = swapped(send.astype(LOW), "rows", 2)
        grad = keep + got.astype(WIDE)
        grad_low = grad.astype(LOW)
        if turn > 0 and nfeat > 2:
            grad_low, rest = tied(grad_low, rest)
        parts = [swapped(grad_low, "rows", z) for z in near[1:]]
        if turn > 0 and nfeat > 2:
            *parts, rest = tied(*parts, lax.ppermute(rest, "feat", along))
            incoming = incoming + rest.astype(WIDE)
        for step, got in enumerate(parts, 1):
            got = got.astype(WIDE)
            grad = grad + jnp.concatenate(
                [got[(slot ^ step) * own:((slot ^ step) + 1) * own] for slot in range(outer)], axis=0
            )
        pair = jnp.concatenate(split(jnp.concatenate([grad, grad[:own]], axis=0)), axis=1)
        part = lax.dot_general(inverse_low, pair, contract, preferred_element_type=WIDE)
        part = part[:, :classes] + part[:, classes:]
        keep, send = halved(part)
        part = keep + swapped(send.astype(LOW), "rows", 1).astype(WIDE)
        top, bottom = halved(part)
        delta = part + swapped(jnp.concatenate([bottom, top]).astype(LOW), "rows", 2).astype(WIDE)
        delta_low = delta.astype(LOW)
        slots = [delta_low] + [swapped(delta_low, "rows", z) for z in near[1:]]
        delta_low = jnp.concatenate([s[:own] for s in slots] + [s[own:] for s in slots], axis=0)
        change = product(delta_low)
        outgoing = incoming - change
        active = actives[turn]
        delta_kept = jnp.where(active, delta[:own], delta_kept)
        if turn < nfeat - 1 and nfeat == 2:
            sent = jnp.where(actives[0], change + fit_rest.astype(WIDE), fit_rest.astype(WIDE))
            got = lax.ppermute(sent.astype(LOW), "feat", along).astype(WIDE)
            outgoing = outgoing - got
            incoming = incoming - got
            incoming_low = incoming.astype(LOW)
        elif turn < nfeat - 1:
            high, rest = split(outgoing)
            incoming_low = lax.ppermute(high, "feat", along)
            incoming = incoming_low.astype(WIDE)
        kept = jnp.where(active, outgoing, kept)

    kept = lax.optimization_barrier(kept)
    squares = jnp.sum(kept * kept, axis=0, keepdims=True)
    squares = lax.all_to_all(
        jnp.broadcast_to(squares[None], (nrows, 1, classes)), "rows", 0, 0, tiled=True
    )
    return (coeffs + delta_kept, kept[None], jnp.sum(squares, axis=0))


def solution(mesh):
    placed = (P("rows", "feat"), P(("feat", "rows"), None), P(("feat", "rows"), None), P("rows"))
    return jax.shard_map(
        on_device,
        mesh=mesh,
        in_specs=placed,
        out_specs=(P(("feat", "rows"), None), P("feat", "rows", None), P("feat", None)),
        check_vma=False,
    )
```

```python
import functools

import jax
import jax.numpy as jnp
from jax import lax
from jax.experimental import pallas as pl
from jax.experimental.pallas import tpu as pltpu
from jax.sharding import PartitionSpec as P

LOW = jnp.bfloat16
WIDE = jnp.float32
INNER = 4


def swapped(shard, axis, bit):
    peers = lax.axis_size(axis)
    return lax.ppermute(shard, axis, [(i, i ^ bit) for i in range(peers)])


def split(wide):
    high = lax.reduce_precision(wide, 8, 7)
    return high.astype(LOW), (wide - high).astype(LOW)


def tied(*arrays):
    return lax.optimization_barrier(arrays)


def halved(whole):
    half = whole.shape[0] // 2
    return whole[:half], whole[half:]


def reorder_kernel(order, own, me_ref, given, near, far, sems):
    me = me_ref[0]
    half = len(order) // 2
    copies = []
    for slot, code in enumerate(order):
        start = pl.multiple_of((me ^ code) * own, own)
        place = pl.ds(slot % half * own, own)
        taken = (near if slot < half else far).at[:, place]
        copies.append(pltpu.make_async_copy(given.at[:, pl.ds(start, own)], taken, sems.at[slot]))
    for copy in copies:
        copy.start()
    for copy in copies:
        copy.wait()


def reordered(features, me, order, own):
    samples, width = features.shape
    half = width // 2
    if own % 128:
        column = jnp.arange(width)
        source = (me ^ jnp.repeat(jnp.array(order), own)) * own + column % own
        pick = (column[:, None] == source[None, :]).astype(LOW)
        taken = jnp.dot(features, pick, preferred_element_type=WIDE).astype(LOW)
        return taken[:, :half], taken[:, half:]
    return pl.pallas_call(
        functools.partial(reorder_kernel, order, own),
        out_shape=[jax.ShapeDtypeStruct((samples, half), features.dtype)] * 2,
        in_specs=[pl.BlockSpec(memory_space=pltpu.SMEM), pl.BlockSpec(memory_space=pl.ANY)],
        out_specs=[pl.BlockSpec(memory_space=pl.ANY)] * 2,
        scratch_shapes=[pltpu.SemaphoreType.DMA((len(order),))],
        compiler_params=pltpu.CompilerParams(vmem_limit_bytes=48 << 20),
        cost_estimate=pl.CostEstimate(flops=0, bytes_accessed=2 * features.size * 2, transcendentals=0),
    )(me.astype(jnp.int32)[None], features)


def on_device(features, coeffs, inverse, labels):
    nfeat = lax.axis_size("feat")
    nrows = lax.axis_size("rows")
    block = lax.axis_index("feat")
    me = lax.axis_index("rows")
    own, classes = coeffs.shape
    outer = nrows // INNER
    near = [z * INNER for z in range(outer)]
    quad = [0, 2, 1, 3]
    order = [q + z for q in quad for z in near]

    def picked(array, codes, axis):
        parts = [lax.dynamic_slice_in_dim(array, (me ^ code) * own, own, axis) for code in codes]
        return jnp.concatenate(parts, axis=axis)

    def over_outer(mine):
        return jnp.concatenate([mine] + [swapped(mine, "rows", z) for z in near[1:]], axis=0)

    def over_bit(mine, bit):
        return jnp.concatenate([mine, swapped(mine, "rows", bit)], axis=0)

    wide_coeffs, *actives = tied(coeffs, *[block == turn for turn in range(nfeat)])
    blocks = [picked(inverse, [z + q for q in quad], 1).astype(LOW) for z in near]

    def product(rows):
        far = swapped(rows, "rows", 1)
        first, far = tied(jnp.dot(keeping, rows, preferred_element_type=WIDE), far)
        return first + jnp.dot(sending, far, preferred_element_type=WIDE)


    keeping, sending = reordered(features, me, order, own)
    near_coeffs, keeping, *blocks = tied(over_outer(wide_coeffs), keeping, *blocks)
    near_coeffs = over_bit(near_coeffs.astype(LOW), 2)

    def product(rows):
        far = swapped(rows, "rows", 1)
        first, far = tied(jnp.dot(keeping, rows, preferred_element_type=WIDE), far)
        return first + jnp.dot(sending, far, preferred_element_type=WIDE)


    inverse_low = jnp.concatenate(
        [blocks[0]] + [swapped(sent, "rows", z) for sent, z in zip(blocks[1:], near[1:])], axis=0
    )
    fitted = product(near_coeffs)
    targets = (labels[:, None] == jnp.arange(classes, dtype=jnp.int32)[None, :]).astype(WIDE)
    if nfeat == 2:
        fit_high, fit_rest = split(fitted)
        fit_high, inverse = tied(fit_high, inverse)
        fit_high, inverse_low = tied(swapped(fit_high, "feat", 1), inverse_low)
        incoming = (targets - fitted) - fit_high.astype(WIDE)
    else:
        for bit in [1 << k for k in range((nfeat - 1).bit_length())]:
            fitted = fitted + swapped(fitted, "feat", bit)
        incoming = targets - fitted
    incoming_low = incoming.astype(LOW)

    own_rest = split(picked(inverse, [z + q for q in quad for z in near[:1]], 1))[1]
    inverse_low = jnp.concatenate([inverse_low, own_rest], axis=0)

    contract = (((0,), (0,)), ((), ()))
    along = [(i, (i + 1) % nfeat) for i in range(nfeat)]
    rest = None
    kept = jnp.zeros_like(incoming)
    delta_kept = jnp.zeros_like(coeffs)
    for turn in range(nfeat):
        send = lax.dot_general(sending, incoming_low, contract, preferred_element_type=WIDE)
        grad = lax.dot_general(keeping, incoming_low, contract, preferred_element_type=WIDE)
        grad, got = tied(grad, swapped(send.astype(LOW), "rows", 1))
        grad = grad + got.astype(WIDE)
        keep, send = halved(grad)
        got = swapped(send.astype(LOW), "rows", 2)
        grad = keep + got.astype(WIDE)
        grad_low = grad.astype(LOW)
        if turn > 0 and nfeat > 2:
            grad_low, rest = tied(grad_low, rest)
        parts = [swapped(grad_low, "rows", z) for z in near[1:]]
        if turn > 0 and nfeat > 2:
            *parts, rest = tied(*parts, lax.ppermute(rest, "feat", along))
            incoming = incoming + rest.astype(WIDE)
        for step, got in enumerate(parts, 1):
            got = got.astype(WIDE)
            grad = grad + jnp.concatenate(
                [got[(slot ^ step) * own:((slot ^ step) + 1) * own] for slot in range(outer)], axis=0
            )
        pair = jnp.concatenate(split(jnp.concatenate([grad, grad[:own]], axis=0)), axis=1)
        part = lax.dot_general(inverse_low, pair, contract, preferred_element_type=WIDE)
        part = part[:, :classes] + part[:, classes:]
        keep, send = halved(part)
        part = keep + swapped(send, "rows", 1)
        top, bottom = halved(swapped(part.astype(LOW), "rows", 2))
        delta = part + jnp.concatenate([bottom, top]).astype(WIDE)
        delta_low = delta.astype(LOW)
        slots = [delta_low] + [swapped(delta_low, "rows", z) for z in near[1:]]
        delta_low = jnp.concatenate([s[:own] for s in slots] + [s[own:] for s in slots], axis=0)
        change = product(delta_low)
        outgoing = incoming - change
        active = actives[turn]
        delta_kept = jnp.where(active, delta[:own], delta_kept)
        if turn < nfeat - 1 and nfeat == 2:
            sent = jnp.where(actives[0], change + fit_rest.astype(WIDE), fit_rest.astype(WIDE))
            got = lax.ppermute(sent.astype(LOW), "feat", along).astype(WIDE)
            outgoing = outgoing - got
            incoming = incoming - got
            incoming_low = incoming.astype(LOW)
        elif turn < nfeat - 1:
            high, rest = split(outgoing)
            incoming_low = lax.ppermute(high, "feat", along)
            incoming = incoming_low.astype(WIDE)
        kept = jnp.where(active, outgoing, kept)

    kept = lax.optimization_barrier(kept)
    squares = jnp.sum(kept * kept, axis=0, keepdims=True)
    squares = lax.all_to_all(
        jnp.broadcast_to(squares[None], (nrows, 1, classes)), "rows", 0, 0, tiled=True
    )
    return (coeffs + delta_kept, kept[None], jnp.sum(squares, axis=0))


def solution(mesh):
    placed = (P("rows", "feat"), P(("feat", "rows"), None), P(("feat", "rows"), None), P("rows"))
    return jax.shard_map(
        on_device,
        mesh=mesh,
        in_specs=placed,
        out_specs=(P(("feat", "rows"), None), P("feat", "rows", None), P("feat", None)),
        check_vma=False,
    )
```
